512 devices in a mesh: row: 32 (over z, y_hi), col: 16 (over x, y_lo, core).
Axes of the slice: x: 4, y: 4 (y_hi: 2, y_lo: 2; y = y_hi * 2 + y_lo), z: 16, core: 2. Of those that a mesh axis runs over, the one named last changes fastest.
Arguments:
- blocks: float32 [32, 16, 8, 128, 128], P('row', 'col'), may hold values from -1.2 to 1.2
- block_rows: int32 [32, 16, 8], P('row', 'col'), may hold values from -1 to 15, as said below
- block_cols: int32 [32, 16, 8], P('row', 'col'), may hold values from -1 to 31, as said below
Outputs:
- square_part: float32 [32, 16, 8, 128, 128], P('row', 'col')
The draws below stay inside these ranges and needn't reach their ends.
Inputs may be any that keep to these rules, and one draw needn't show every extreme that they name: Empty slots have -1 in block_rows and block_cols alike; a used slot has a block row below 16; no block is listed twice in one tile. At most 4 used slots of one tile share a block row, and some tile has a block row with exactly 4. Some tile uses all 8 slots, and some tile has empty slots. `block_cols`: the two lists describe the same slots; a used slot has a block column below 32.
All inputs are finite; a program needn't handle non-finite values.
Results may differ from the reference program's by a relative error of at most 0.0003.
Values sent between devices are 32-bit elements; how exact they have to be, the bound alone decides.
A program may use at most 64 MiB of HBM per device.

```python
import jax
import jax.numpy as jnp
from jax import lax

BS = 128
NBLK = 512
ACT = 2
SECTIONS = 4
TILE_ROWS = 32
TILE_COLS = 16
RB = 16
CB = 32
SLOTS = 8
QMAX = 4
N_ROW = 32
N_COL = 16


def block_pattern(key):
    base = jax.random.fold_in(key, 47)
    keys = jax.random.split(base, 8)
    reach = max(NBLK // 56, 2)
    tile_count = N_ROW * N_COL
    span = RB * CB
    order = jax.random.permutation(keys[0], NBLK).astype(jnp.int32)
    distance = jnp.abs(order[:, None] - order[None, :])
    coin = jax.random.randint(keys[1], (NBLK, NBLK), 0, reach + 1).astype(jnp.int32)
    band = (distance <= reach) & (coin >= distance)
    identity = jnp.arange(NBLK, dtype=jnp.int32)
    diagonal = identity[:, None] == identity[None, :]
    band_tiles = band.reshape(N_ROW, RB, N_COL, CB).transpose(0, 2, 1, 3)
    diagonal_tiles = diagonal.reshape(N_ROW, RB, N_COL, CB).transpose(0, 2, 1, 3)
    forced_flat = jax.random.randint(keys[2], (), 0, tile_count).astype(jnp.int32)
    sparse_flat = (forced_flat + 1 + jax.random.randint(keys[3], (), 0, tile_count - 1).astype(jnp.int32)) % tile_count
    tile_flat = jnp.arange(tile_count, dtype=jnp.int32).reshape(N_ROW, N_COL)
    forced_tile = tile_flat == forced_flat
    first_row = RB - 1 - jax.random.randint(keys[4], (), 0, ACT).astype(jnp.int32)
    local_rows = jnp.arange(RB, dtype=jnp.int32)
    offset_rows = (local_rows - first_row) % RB
    in_forced_row = offset_rows < ACT
    column_perms = jax.vmap(lambda one: jax.random.permutation(one, CB))(jax.random.split(keys[5], ACT)).astype(jnp.int32)
    column_perms = (column_perms + (CB - 1 - column_perms[:, 0:1])) % CB
    column_ranks = jnp.argsort(column_perms, axis=1).astype(jnp.int32)
    row_ranks = column_ranks[jnp.minimum(offset_rows, ACT - 1)]
    forced_local = in_forced_row[:, None] & (row_ranks < QMAX)
    forced = forced_tile[:, :, None, None] & forced_local[None, None, :, :]
    live = band_tiles | forced
    tiebreak = jax.vmap(lambda one: jax.random.permutation(one, span))(jax.random.split(keys[6], tile_count))
    tiebreak = tiebreak.astype(jnp.int32).reshape(N_ROW, N_COL, RB, CB)
    kind = jnp.where(forced, 0, jnp.where(diagonal_tiles, 1, 2)).astype(jnp.int32)
    score = jnp.where(live, kind * span + tiebreak, 3 * span + tiebreak)
    row_order = jnp.argsort(score, axis=-1).astype(jnp.int32)
    row_place = jnp.argsort(row_order, axis=-1).astype(jnp.int32)
    kept = live & (row_place < QMAX)
    tile_score = jnp.where(kept, score, 3 * span + tiebreak).reshape(N_ROW, N_COL, span)
    picked = jnp.argsort(tile_score, axis=-1).astype(jnp.int32)[:, :, :SLOTS]
    used = jnp.take_along_axis(kept.reshape(N_ROW, N_COL, span), picked, axis=-1)
    limit = jnp.where(tile_flat == sparse_flat, SLOTS // 2, SLOTS).astype(jnp.int32)
    used = used & (jnp.arange(SLOTS, dtype=jnp.int32)[None, None, :] < limit[:, :, None])
    rows_out = jnp.where(used, picked // CB, -1).astype(jnp.int32)
    cols_out = jnp.where(used, picked % CB, -1).astype(jnp.int32)
    shuffles = jax.vmap(lambda one: jax.random.permutation(one, SLOTS))(jax.random.split(keys[7], tile_count))
    shuffles = shuffles.astype(jnp.int32).reshape(N_ROW, N_COL, SLOTS)
    return (jnp.take_along_axis(rows_out, shuffles, axis=-1), jnp.take_along_axis(cols_out, shuffles, axis=-1))


def draw_block_rows(key, part):
    return block_pattern(key)[0].astype(jnp.int32)


def draw_block_cols(key, part):
    return block_pattern(key)[1].astype(jnp.int32)


def block_levels(key, extent, cuts, least, top_value):
    def one(axis_at, shards_of):
        draws = jax.random.uniform(jax.random.fold_in(jax.random.fold_in(key, 6), axis_at), (shards_of,), jnp.float32, least / len(cuts), top_value / len(cuts))
        return jnp.repeat(jnp.exp(draws), extent[axis_at] // shards_of).reshape((-1,) + (1,) * (len(extent) - axis_at - 1))

    factor_of = one(*cuts[0])
    for cut in cuts[1:]:
        factor_of = factor_of * one(*cut)
    return factor_of


def scatter_about(key, extent, scale, most, pieces=(), held_as=jnp.bfloat16):
    array = scale * jax.random.normal(key, extent, jnp.float32)
    if pieces:
        array = array * block_levels(key, extent, pieces, -0.22, 0.18)
    return jnp.clip(array, -most, most).astype(held_as)


def setup_inputs(seed: int = 0) -> dict:
    splits = jax.random.split(jax.random.key(seed), 4)
    blocks = scatter_about(splits[0], (TILE_ROWS, TILE_COLS, SLOTS, BS, BS), 0.2, 1.2, ((0, 32), (1, 16)), jnp.float32)
    block_rows = draw_block_rows(jax.random.fold_in(splits[3], 71), 0)
    block_cols = draw_block_cols(jax.random.fold_in(splits[3], 71), 0)
    return {"blocks": blocks, "block_rows": block_rows, "block_cols": block_cols}


def section_product(panel, pair, out_rows, out_cols, depth):
    panel_vals, panel_rows, panel_cols = panel
    pair_vals, pair_inner, pair_cols = pair
    panel_iota = jnp.arange(panel_rows.shape[0], dtype=jnp.int32)
    pair_iota = jnp.arange(pair_inner.shape[0], dtype=jnp.int32)
    depth_iota = jnp.arange(depth, dtype=jnp.int32)
    panel_live = panel_rows >= 0
    earlier = (panel_rows[None, :] == panel_rows[:, None]) & panel_live[None, :] & (panel_iota[None, :] < panel_iota[:, None])
    within = jnp.sum(earlier.astype(jnp.int32), axis=1)
    picked = (panel_rows[None, None, :] == out_rows[:, None, None]) & (within[None, None, :] == depth_iota[None, :, None])
    picked = picked & panel_live[None, None, :] & (out_rows >= 0)[:, None, None]
    picked_int = picked.astype(jnp.int32)
    panel_slot = jnp.sum(picked_int * panel_iota[None, None, :], axis=2)
    found = jnp.sum(picked_int, axis=2) > 0
    inner = jnp.sum(picked_int * panel_cols[None, None, :], axis=2)
    matched = (pair_inner[None, None, :] == inner[:, :, None]) & (pair_cols[None, None, :] == out_cols[:, None, None])
    matched = matched & (pair_inner >= 0)[None, None, :] & found[:, :, None]
    matched_int = matched.astype(jnp.int32)
    pair_slot = jnp.sum(matched_int * pair_iota[None, None, :], axis=2)
    weight = (jnp.sum(matched_int, axis=2) > 0).astype(jnp.float32)
    left = panel_vals[panel_slot] * weight[:, :, None, None]
    right = pair_vals[pair_slot]
    return jnp.einsum("tqij,tqjk->tik", left, right, precision=lax.Precision.HIGHEST, preferred_element_type=jnp.float32)


def make_pair(first, second, row_span):
    inner = jnp.concatenate([first[1], jnp.where(second[1] >= 0, second[1] + row_span, -1)])
    return (jnp.concatenate([first[0], second[0]]), inner, jnp.concatenate([first[2], second[2]]))


def reference(blocks, block_rows, block_cols):
    row_span = NBLK // N_ROW

    def one_tile(flat):
        row_index = flat // N_COL
        col_index = flat % N_COL
        total = jnp.zeros((SLOTS, BS, BS), jnp.float32)
        for section in range(SECTIONS):
            root = (row_index // 2 + section) % N_COL
            panel = (blocks[row_index, root], block_rows[row_index, root], block_cols[row_index, root])
            upper = 2 * root
            first = (blocks[upper, col_index], block_rows[upper, col_index], block_cols[upper, col_index])
            second = (blocks[upper + 1, col_index], block_rows[upper + 1, col_index], block_cols[upper + 1, col_index])
            pair = make_pair(first, second, row_span)
            total = total + section_product(panel, pair, block_rows[row_index, col_index], block_cols[row_index, col_index], 2 * ACT)
        return total

    tiles = lax.map(one_tile, jnp.arange(N_ROW * N_COL, dtype=jnp.int32))
    return tiles.reshape(N_ROW, N_COL, SLOTS, BS, BS)
```

```python
import functools

import jax
import jax.numpy as jnp
from jax import lax
from jax.experimental import pallas as pl
from jax.experimental.pallas import tpu as pltpu
from jax.sharding import PartitionSpec as P

MESH = pl.DeviceIdType.MESH
BS = 128
SLOTS = 8
RB = 16
SECTIONS = 4
VIA_Z = 4
F32 = jnp.float32


def gather_kernel(blocks, rows, cols, b_out, a_out, mb_out, ma_out, meta, local_sem,
                  zs, zr, ys, yr, mzs, mzr, mys, myr, rs, rr, rms, rmr, gs, gr, cs, cr):
    row, col = lax.axis_index("row"), lax.axis_index("col")
    z, yh = row // 2, row % 2
    other = 1 - yh
    x, yl, core = col // 4, (col // 2) % 2, col % 2
    below = ((z + 15) % 16 * 2 + yh, col)
    above = ((z + 1) % 16 * 2 + yh, col)
    partner = (z * 2 + other, col)
    section = (col + 16 - z) % 16
    is_root = section < SECTIONS
    chunk = x * 2 + core

    def remote(src, dst, send, recv, to):
        return pltpu.make_async_remote_copy(
            src_ref=src, dst_ref=dst, send_sem=send, recv_sem=recv, device_id=to, device_id_type=MESH
        )

    own = pltpu.make_async_copy(blocks, b_out.at[0, yh], local_sem.at[0])
    own.start()
    meta[...] = jnp.full((8, BS), -1, jnp.int32)
    meta[0:1, 0:SLOTS] = rows[...]
    meta[1:2, 0:SLOTS] = cols[...]
    own_meta = pltpu.make_async_copy(meta, mb_out.at[0, yh], local_sem.at[1])
    own_meta.start()

    barrier = pltpu.get_barrier_semaphore()
    for to in (below, above, partner):
        pl.semaphore_signal(barrier, inc=1, device_id=to, device_id_type=MESH)
    for d in range(1, 16):
        pl.semaphore_signal(barrier, inc=1, device_id=(row, (col + d) % 16), device_id_type=MESH)
    pl.semaphore_wait(barrier, 18)

    sends = []

    def go(copy):
        copy.start()
        sends.append(copy)

    go(remote(meta, mb_out.at[1, yh], mzs.at[0], mzr.at[0], below))
    go(remote(meta, mb_out.at[0, yh], mys.at[0], myr.at[0], partner))
    for q in range(SLOTS):
        go(remote(blocks.at[q], b_out.at[1, yh, q], zs.at[q], zr.at[q], below))
        go(remote(blocks.at[q], b_out.at[0, yh, q], ys.at[q], yr.at[q], partner))

    def root_copies():
        out = []
        for d in range(1, 16):
            c = (col + d) % 16
            b = c // 4 * 2 + c % 2
            out.append(remote(blocks.at[b], a_out.at[b, section], rs.at[d], rr.at[section], (row, c)))
            out.append(remote(meta, ma_out.at[section], rms.at[d], rmr.at[section], (row, c)))
        return out

    @pl.when(is_root)
    def _():
        for copy in root_copies():
            copy.start()
        mine = pltpu.make_async_copy(blocks.at[chunk], a_out.at[chunk, section], local_sem.at[2])
        mine.start()
        mine_meta = pltpu.make_async_copy(meta, ma_out.at[section], local_sem.at[3])
        mine_meta.start()
        mine.wait()
        mine_meta.wait()

    own.wait()
    own_meta.wait()

    def from_above(i):
        s, q = 1 + i // SLOTS, i % SLOTS
        return remote(blocks.at[q], b_out.at[s, yh, q], zs.at[i], zr.at[i], below)

    def panel_spread():
        for s in range(SECTIONS):
            @pl.when(section != s)
            def _():
                remote(blocks.at[0], a_out.at[chunk, s], rs.at[0], rr.at[s], partner).wait_recv()
                remote(meta, ma_out.at[s], rms.at[0], rmr.at[s], partner).wait_recv()
        for d in range(1, 4):
            to = (row, (x + d) % 4 * 4 + yl * 2 + core)
            go(remote(a_out.at[chunk], a_out.at[chunk], gs.at[d], gr.at[d], to))
        twin = (row, x * 4 + yl * 2 + 1 - core)
        go(remote(a_out.at[chunk], a_out.at[chunk], cs.at[0], cr.at[0], twin))

    def panel_twin():
        twin = (row, x * 4 + yl * 2 + 1 - core)
        for d in range(1, 4):
            b = (x + 4 - d) % 4 * 2 + core
            remote(a_out.at[b], a_out.at[b], gs.at[d], gr.at[d], twin).wait_recv()
            go(remote(a_out.at[b], a_out.at[b], cs.at[d], cr.at[d], twin))

    for i in range(24):
        s, q = 1 + i // SLOTS, i % SLOTS
        if q == 0:
            remote(meta, mb_out.at[s, yh], mzs.at[s - 1], mzr.at[s - 1], below).wait_recv()
            if s < SECTIONS - 1:
                go(remote(mb_out.at[s, yh], mb_out.at[s + 1, yh], mzs.at[s], mzr.at[s], below))
            go(remote(mb_out.at[s, yh], mb_out.at[s, yh], mys.at[s], myr.at[s], partner))
        from_above(i).wait_recv()
        if s < SECTIONS - 1:
            go(remote(b_out.at[s, yh, q], b_out.at[s + 1, yh, q], zs.at[i + 8], zr.at[i + 8], below))
        if s < SECTIONS - 1 or q < SLOTS - VIA_Z:
            go(remote(b_out.at[s, yh, q], b_out.at[s, yh, q], ys.at[s * 8 + q], yr.at[s * 8 + q], partner))
        if i == 10:
            panel_spread()

    def from_partner(s, q):
        return remote(blocks.at[q], b_out.at[s, other, q], ys.at[s * 8 + q], yr.at[s * 8 + q], partner)

    for v in range(VIA_Z):
        q = SLOTS - VIA_Z + v
        from_partner(2, q).wait_recv()
        go(remote(b_out.at[2, other, q], b_out.at[3, other, q], zs.at[24 + v], zr.at[24 + v], below))
    panel_twin()
    for s in range(SECTIONS):
        remote(meta, mb_out.at[s, other], mys.at[s], myr.at[s], partner).wait_recv()
        for q in range(SLOTS):
            if s == 2 and q >= SLOTS - VIA_Z:
                continue
            if s == 3 and q >= SLOTS - VIA_Z:
                v = q - (SLOTS - VIA_Z)
                remote(blocks.at[q], b_out.at[3, other, q], zs.at[24 + v], zr.at[24 + v], below).wait_recv()
            else:
                from_partner(s, q).wait_recv()
    twin = (row, x * 4 + yl * 2 + 1 - core)
    for d in range(4):
        b = (x + 4 - d) % 4 * 2 + 1 - core
        remote(a_out.at[b], a_out.at[b], cs.at[d], cr.at[d], twin).wait_recv()

    @pl.when(is_root)
    def _():
        for copy in root_copies():
            copy.wait_send()

    for copy in sends:
        copy.wait_send()


def product_kernel(rows, cols, b_in, a_in, mb, ma, out, table, table_s, sem):
    n = SLOTS
    diag = lax.broadcasted_iota(jnp.int32, (n, n), 0) == lax.broadcasted_iota(jnp.int32, (n, n), 1)

    def upright(line):
        wide = jnp.broadcast_to(line, (n, n))
        return jnp.sum(jnp.where(diag, wide, 0), axis=1, keepdims=True)

    out_rows = upright(rows[...])
    out_cols = upright(cols[...])
    for s in range(SECTIONS):
        a_rows = ma[s, 0:1, 0:n]
        a_cols = ma[s, 1:2, 0:n]
        same_row = (out_rows == a_rows) & (out_rows >= 0)
        found = jnp.full((n, n), -1, jnp.int32)
        for h in range(2):
            for q in range(n):
                inner = mb[s, h, 0:1, q:q + 1]
                b_col = mb[s, h, 1:2, q:q + 1]
                hit = (a_cols == inner + RB * h) & (out_cols == b_col) & (inner >= 0)
                found = jnp.where(hit & same_row, h * n + q, found)
        table[s * n:(s + 1) * n, 0:n] = found
    copy = pltpu.make_async_copy(table, table_s, sem)
    copy.start()
    out[...] = jnp.zeros_like(out)
    copy.wait()

    def step(i, carry):
        s, t, p = i // 64, (i // 8) % 8, i % 8
        where = table_s[i // 8, p]

        @pl.when(where >= 0)
        def _():
            a = a_in[p, s]
            b = b_in[s, where // n, where % n]
            a_hi = a.astype(jnp.bfloat16)
            a_lo = (a - a_hi.astype(F32)).astype(jnp.bfloat16)
            b_hi = b.astype(jnp.bfloat16)
            b_lo = (b - b_hi.astype(F32)).astype(jnp.bfloat16)
            left = jnp.concatenate([a_hi, a_lo], axis=1)
            right = jnp.concatenate(
                [jnp.concatenate([b_hi, b_lo], axis=1),
                 jnp.concatenate([b_hi, jnp.zeros_like(b_lo)], axis=1)], axis=0)
            both = jnp.dot(left, right, preferred_element_type=F32)
            out[t] += both[:, :BS] + both[:, BS:]

        return carry

    lax.fori_loop(0, SECTIONS * n * n, step, 0)


def body(blocks, block_rows, block_cols):
    x = blocks[0, 0]
    rows, cols = block_rows[0], block_cols[0]
    dma = pltpu.SemaphoreType.DMA
    hbm = pl.BlockSpec(memory_space=pl.ANY)
    vmem = pl.BlockSpec(memory_space=pltpu.VMEM)
    b_all, a_all, mb, ma = pl.pallas_call(
        gather_kernel,
        out_shape=(
            jax.ShapeDtypeStruct((SECTIONS, 2, SLOTS, BS, BS), F32),
            jax.ShapeDtypeStruct((SLOTS, SECTIONS, BS, BS), F32),
            jax.ShapeDtypeStruct((SECTIONS, 2, 8, BS), jnp.int32),
            jax.ShapeDtypeStruct((SECTIONS, 8, BS), jnp.int32),
        ),
        in_specs=[hbm, vmem, vmem],
        out_specs=(hbm, hbm, hbm, hbm),
        scratch_shapes=[
            pltpu.VMEM((8, BS), jnp.int32), dma((4,)),
            dma((28,)), dma((28,)), dma((32,)), dma((32,)),
            dma((3,)), dma((3,)), dma((4,)), dma((4,)),
            dma((16,)), dma((4,)), dma((16,)), dma((4,)),
            dma((4,)), dma((4,)), dma((4,)), dma((4,)),
        ],
        compiler_params=pltpu.CompilerParams(collective_id=0, has_side_effects=True),
        name="gather_tiles",
    )(x, rows, cols)
    out = pl.pallas_call(
        product_kernel,
        out_shape=jax.ShapeDtypeStruct((SLOTS, BS, BS), F32),
        in_specs=[vmem] * 6,
        out_specs=vmem,
        scratch_shapes=[
            pltpu.VMEM((SECTIONS * SLOTS, BS), jnp.int32),
            pltpu.SMEM((SECTIONS * SLOTS, BS), jnp.int32),
            dma(()),
        ],
        compiler_params=pltpu.CompilerParams(vmem_limit_bytes=32 * 2**20),
        name="matched_products",
    )(rows, cols, b_all, a_all, mb, ma)
    return out[None, None]


def solution(mesh):
    return jax.shard_map(
        body,
        mesh=mesh,
        in_specs=(P("row", "col", None, None, None), P("row", "col", None), P("row", "col", None)),
        out_specs=P("row", "col", None, None, None),
        check_vma=False,
    )
```

```python
import jax
import jax.numpy as jnp
from jax import lax
from jax.experimental import pallas as pl
from jax.experimental.pallas import tpu as pltpu
from jax.sharding import PartitionSpec as P

MESH = pl.DeviceIdType.MESH
BS = 128
SLOTS = 8
RB = 16
SECTIONS = 4
DEPTH = 4
F32 = jnp.float32
BF16 = jnp.bfloat16


def kernel(blocks, rows, cols, out, rows_v, cols_v, meta, mb, ma, mc, b0, b1, b2, a_all, c_down, c_in, acc,
           table, table_s, local_sem, ready, zs, zr, ys, yr, mzs, mzr, mys, myr, mus, mur,
           rs, rr, rms, rmr, gs, gr, cs, cr, out_sem):
    row, col = lax.axis_index("row"), lax.axis_index("col")
    z, yh = row // 2, row % 2
    other = 1 - yh
    x, yl, core = col // 4, (col // 2) % 2, col % 2
    row_below, row_above = (z + 15) % 16 * 2 + yh, (z + 1) % 16 * 2 + yh
    below, above = (row_below, col), (row_above, col)
    partner = (z * 2 + other, col)
    twin = (row, x * 4 + yl * 2 + 1 - core)
    section = (col + 16 - z) % 16
    chunk = x * 2 + core
    line = [(row, (x + d) % 4 * 4 + yl * 2 + core) for d in range(1, 4)]

    def remote(src, dst, send, recv, to):
        return pltpu.make_async_remote_copy(
            src_ref=src, dst_ref=dst, send_sem=send, recv_sem=recv, device_id=to, device_id_type=MESH
        )

    def signal(sem, to):
        pl.semaphore_signal(sem, inc=1, device_id=to, device_id_type=MESH)

    barrier = pltpu.get_barrier_semaphore()
    for to in (below, partner, twin, *line):
        signal(barrier, to)
    for s in range(3):
        @pl.when(section != s)
        def _():
            signal(barrier, (row, (z + s) % 16))
    signal(barrier, (row_below, (z + 2) % 16))

    own = pltpu.make_async_copy(blocks, b0.at[yh], local_sem.at[0])
    own.start()
    own_rows = pltpu.make_async_copy(rows, rows_v, local_sem.at[1])
    own_rows.start()
    own_cols = pltpu.make_async_copy(cols, cols_v, local_sem.at[2])
    own_cols.start()
    a_all[SLOTS] = jnp.zeros((SECTIONS, BS, BS), F32)
    meta[...] = jnp.full((8, BS), -1, jnp.int32)
    own_rows.wait()
    own_cols.wait()
    meta[0:1, 0:SLOTS] = rows_v[...]
    meta[1:2, 0:SLOTS] = cols_v[...]
    mb[0, yh] = meta[...]
    own.wait()

    pl.semaphore_wait(barrier, 6 + jnp.where(section < 3, 15, jnp.where(section == 3, 16, 0)))
    signal(ready, above)

    sends = []

    def go(copy):
        copy.start()
        sends.append(copy)

    go(remote(meta, mb.at[0, yh], mys.at[0], myr.at[0], partner))
    go(remote(meta, mc, mus, mur, above))
    for q in range(SLOTS):
        go(remote(b0.at[yh, q], b0.at[yh, q], ys.at[q], yr.at[q], partner))

    def root_copies(d, last):
        c = (col + d) % 16
        b = c // 4 * 2 + c % 2
        to = (row_above if last else row, c)
        s = SECTIONS - 1 if last else section
        return (
            remote(meta, ma.at[s], rms.at[d], rmr.at[s], to),
            remote(blocks.at[b], a_all.at[b, s], rs.at[d], rr.at[s], to),
        )

    def each_root_copy(act):
        @pl.when(section < 3)
        def _():
            for d in range(1, 16):
                for copy in root_copies(d, False):
                    act(copy)

        @pl.when(section == 3)
        def _():
            for d in range(16):
                for copy in root_copies(d, True):
                    act(copy)

    each_root_copy(lambda copy: copy.start())

    pl.semaphore_wait(ready, 1)
    go(remote(meta, mb.at[1, yh], mzs.at[0], mzr.at[0], below))
    for q in range(SLOTS):
        go(remote(b0.at[yh, q], b1.at[yh, q], zs.at[q], zr.at[q], below))

    @pl.when(section < 3)
    def _():
        mine = pltpu.make_async_copy(blocks.at[chunk], a_all.at[chunk, section], local_sem.at[3])
        mine.start()
        ma[section] = meta[...]
        mine.wait()

    remote(meta, mb.at[1, yh], mzs.at[0], mzr.at[0], below).wait_recv()
    go(remote(mb.at[1, yh], mb.at[2, yh], mzs.at[1], mzr.at[1], below))
    go(remote(mb.at[1, yh], mb.at[1, yh], mys.at[1], myr.at[1], partner))
    for q in range(SLOTS):
        remote(b0.at[yh, q], b1.at[yh, q], zs.at[q], zr.at[q], below).wait_recv()
        go(remote(b1.at[yh, q], b2.at[yh, q], zs.at[8 + q], zr.at[8 + q], below))
    remote(meta, mb.at[2, yh], mzs.at[1], mzr.at[1], below).wait_recv()
    go(remote(mb.at[2, yh], mb.at[2, yh], mys.at[2], myr.at[2], partner))

    for s in range(SECTIONS):
        def arrived():
            remote(meta, ma.at[s], rms.at[0], rmr.at[s], partner).wait_recv()
            remote(blocks.at[0], a_all.at[0, s], rs.at[0], rr.at[s], partner).wait_recv()

        if s < 3:
            pl.when(section != s)(arrived)
        else:
            arrived()
    for d in range(1, 4):
        go(remote(a_all.at[chunk], a_all.at[chunk], gs.at[d], gr.at[d], line[d - 1]))
    go(remote(a_all.at[chunk], a_all.at[chunk], cs.at[0], cr.at[0], twin))

    for q in range(SLOTS):
        remote(b1.at[yh, q], b2.at[yh, q], zs.at[8 + q], zr.at[8 + q], below).wait_recv()
        go(remote(b2.at[yh, q], b2.at[yh, q], ys.at[8 + q], yr.at[8 + q], partner))
    for q in range(SLOTS):
        go(remote(b1.at[yh, q], b1.at[yh, q], ys.at[16 + q], yr.at[16 + q], partner))
    for d in range(1, 4):
        b = (x + 4 - d) % 4 * 2 + core
        remote(a_all.at[b], a_all.at[b], gs.at[d], gr.at[d], twin).wait_recv()
        go(remote(a_all.at[b], a_all.at[b], cs.at[d], cr.at[d], twin))

    for i in range(3):
        remote(meta, mb.at[i, other], mys.at[i], myr.at[i], partner).wait_recv()
    remote(meta, mc, mus, mur, above).wait_recv()
    n = SLOTS
    lane = lax.broadcasted_iota(jnp.int32, (n, n), 1)
    diag = lax.broadcasted_iota(jnp.int32, (n, n), 0) == lane

    def upright(values):
        wide = jnp.broadcast_to(values, (n, n))
        return jnp.sum(jnp.where(diag, wide, 0), axis=1, keepdims=True)

    for s, (lists, i) in enumerate(((meta, 0), (meta, 1), (meta, 2), (mc, 2))):
        out_rows, out_cols = upright(lists[0:1, 0:n]), upright(lists[1:2, 0:n])
        a_rows, a_cols = ma[s, 0:1, 0:n], ma[s, 1:2, 0:n]
        same_row = (out_rows == a_rows) & (out_rows >= 0)
        found = jnp.full((n, n), -1, jnp.int32)
        for h in range(2):
            for q in range(n):
                inner, b_col = mb[i, h, 0:1, q:q + 1], mb[i, h, 1:2, q:q + 1]
                hit = (a_cols == inner + RB * h) & (out_cols == b_col) & (inner >= 0)
                found = jnp.where(hit, h * n + q, found)
        found = jnp.where(same_row, found, -1)
        matched = jnp.where(found >= 0, 1, 0)
        rank = jnp.zeros((n, n), jnp.int32)
        for p in range(n - 1):
            rank = rank + jnp.where(lane > p, matched[:, p:p + 1], 0)
        for d in range(DEPTH):
            pick = (matched > 0) & (rank == d)
            a_at = n + jnp.sum(jnp.where(pick, lane - n, 0), axis=1, keepdims=True)
            b_at = jnp.sum(jnp.where(pick, found, 0), axis=1, keepdims=True)
            table[s * n:(s + 1) * n, d:d + 1] = a_at
            table[s * n:(s + 1) * n, DEPTH + d:DEPTH + d + 1] = b_at
    to_scalars = pltpu.make_async_copy(table, table_s, local_sem.at[4])
    to_scalars.start()
    to_scalars.wait()

    for d in range(4):
        b = (x + 4 - d) % 4 * 2 + 1 - core
        remote(a_all.at[b], a_all.at[b], cs.at[d], cr.at[d], twin).wait_recv()

    def halves(v):
        high = v.astype(BF16)
        return high, (v - high.astype(F32)).astype(BF16)

    def product(s, t, b_ref):
        lefts, rights = [], []
        for d in range(DEPTH):
            a = a_all[table_s[s * n + t, d], s]
            at = table_s[s * n + t, DEPTH + d]
            b = b_ref[at // n, at % n]
            lefts += halves(a)
            wide = jnp.concatenate(halves(b), axis=1)
            rights += [wide, wide]
        both = jnp.dot(jnp.concatenate(lefts, axis=1), jnp.concatenate(rights, axis=0), preferred_element_type=F32)
        return both[:, :BS] + both[:, BS:]

    def partner_blocks(ref, first):
        for q in range(SLOTS):
            remote(ref.at[other, q], ref.at[other, q], ys.at[first + q], yr.at[first + q], partner).wait_recv()

    def down(t):
        return remote(c_down.at[t], c_in.at[t], zs.at[16 + t], zr.at[16 + t], below)

    partner_blocks(b2, 8)

    def last_section(t, carry):
        c_down[t] = product(3, t, b2)
        down(t).start()
        return carry

    lax.fori_loop(0, SLOTS, last_section, 0)
    partner_blocks(b0, 0)

    def early_sections(t, carry):
        acc[t] = product(0, t, b0) + product(2, t, b2)
        return carry

    lax.fori_loop(0, SLOTS, early_sections, 0)
    partner_blocks(b1, 16)

    def late_section(t, carry):
        acc[t] += product(1, t, b1)
        return carry

    lax.fori_loop(0, SLOTS, late_section, 0)

    def result(t):
        return pltpu.make_async_copy(acc.at[t], out.at[t], out_sem.at[t])

    def finish(t, carry):
        down(t).wait_recv()
        acc[t] += c_in[t]
        result(t).start()
        return carry

    lax.fori_loop(0, SLOTS, finish, 0)
    for t in range(SLOTS):
        down(t).wait_send()
    each_root_copy(lambda copy: copy.wait_send())
    for copy in sends:
        copy.wait_send()
    for t in range(SLOTS):
        result(t).wait()


def body(blocks, block_rows, block_cols):
    dma = pltpu.SemaphoreType.DMA
    hbm = pl.BlockSpec(memory_space=pl.ANY)
    tile = pltpu.VMEM((2, SLOTS, BS, BS), F32)
    lists = (8, BS)
    i32 = jnp.int32
    out = pl.pallas_call(
        kernel,
        out_shape=jax.ShapeDtypeStruct((SLOTS, BS, BS), F32),
        in_specs=[hbm, hbm, hbm],
        out_specs=hbm,
        scratch_shapes=[
            pltpu.VMEM((1, SLOTS), i32), pltpu.VMEM((1, SLOTS), i32),
            pltpu.VMEM(lists, i32), pltpu.VMEM((3, 2, *lists), i32), pltpu.VMEM((SECTIONS, *lists), i32),
            pltpu.VMEM(lists, i32),
            tile, tile, tile,
            pltpu.VMEM((SLOTS + 1, SECTIONS, BS, BS), F32),
            pltpu.VMEM((SLOTS, BS, BS), F32), pltpu.VMEM((SLOTS, BS, BS), F32), pltpu.VMEM((SLOTS, BS, BS), F32),
            pltpu.VMEM((SECTIONS * SLOTS, BS), i32), pltpu.SMEM((SECTIONS * SLOTS, BS), i32),
            dma((5,)), pltpu.SemaphoreType.REGULAR,
            dma((24,)), dma((24,)), dma((24,)), dma((24,)),
            dma((2,)), dma((2,)), dma((3,)), dma((3,)), dma(()), dma(()),
            dma((16,)), dma((4,)), dma((16,)), dma((4,)),
            dma((4,)), dma((4,)), dma((4,)), dma((4,)), dma((SLOTS,)),
        ],
        compiler_params=pltpu.CompilerParams(
            collective_id=0, has_side_effects=True, vmem_limit_bytes=32 * 2**20
        ),
        name="four_sections",
    )(blocks[0, 0], block_rows[0], block_cols[0])
    return out[None, None]


def solution(mesh):
    return jax.shard_map(
        body,
        mesh=mesh,
        in_specs=(P("row", "col", None, None, None), P("row", "col", None), P("row", "col", None)),
        out_specs=P("row", "col", None, None, None),
        check_vma=False,
    )
```

```python
import jax
import jax.numpy as jnp
from jax import lax
from jax.experimental import pallas as pl
from jax.experimental.pallas import tpu as pltpu
from jax.sharding import PartitionSpec as P

MESH = pl.DeviceIdType.MESH
BS = 128
SLOTS = 8
RB = 16
SECTIONS = 4
DEPTH = 4
EARLY = 2
F32 = jnp.float32
BF16 = jnp.bfloat16


def kernel(blocks, rows, cols, out, rows_v, cols_v, meta, mb, ma, mc, b0, b1, b2, a_last, a_mid, a_first, c_down, c_in, acc,
           table, table_s, local_sem, ready, zs, zr, ys, yr, mzs, mzr, mys, myr, mus, mur,
           rs, rr, rms, rmr, ks, kr, gs, gr, cs, cr, out_sem):
    row, col = lax.axis_index("row"), lax.axis_index("col")
    z, yh = row // 2, row % 2
    other = 1 - yh
    x, yl, core = col // 4, (col // 2) % 2, col % 2
    row_below, row_above = (z + 15) % 16 * 2 + yh, (z + 1) % 16 * 2 + yh
    below, above = (row_below, col), (row_above, col)
    partner = (z * 2 + other, col)
    twin = (row, x * 4 + yl * 2 + 1 - core)
    opposite = (row, x * 4 + (1 - yl) * 2 + core)
    section = (col + 16 - z) % 16
    chunk = x * 2 + core
    line = [(row, (x + d) % 4 * 4 + yl * 2 + core) for d in range(1, 4)]

    def remote(src, dst, send, recv, to):
        return pltpu.make_async_remote_copy(
            src_ref=src, dst_ref=dst, send_sem=send, recv_sem=recv, device_id=to, device_id_type=MESH
        )

    def signal(sem, to):
        pl.semaphore_signal(sem, inc=1, device_id=to, device_id_type=MESH)

    barrier = pltpu.get_barrier_semaphore()
    for to in (below, partner, twin, opposite, *line):
        signal(barrier, to)
    for s in range(3):
        @pl.when(section != s)
        def _():
            signal(barrier, (row, (z + s) % 16))
    signal(barrier, (row_below, (z + 2) % 16))

    own = pltpu.make_async_copy(blocks, b0.at[yh], local_sem.at[0])
    own.start()
    own_rows = pltpu.make_async_copy(rows, rows_v, local_sem.at[1])
    own_rows.start()
    own_cols = pltpu.make_async_copy(cols, cols_v, local_sem.at[2])
    own_cols.start()
    for ref in (a_last, a_mid, a_first):
        ref[SLOTS] = jnp.zeros(ref.shape[1:], F32)
    meta[...] = jnp.full((8, BS), -1, jnp.int32)
    own_rows.wait()
    own_cols.wait()
    meta[0:1, 0:SLOTS] = rows_v[...]
    meta[1:2, 0:SLOTS] = cols_v[...]
    mb[0, yh] = meta[...]
    own.wait()

    pl.semaphore_wait(barrier, 7 + jnp.where(section < 3, 15, jnp.where(section == 3, 16, 0)))
    signal(ready, above)

    sends = [], [], []

    def go(copy, when=0):
        copy.start()
        sends[when].append(copy)

    def across(ref, q, first, when=0):
        go(remote(ref.at[yh, q], ref.at[yh, q], ys.at[first + q], yr.at[first + q], partner), when)

    go(remote(meta, mb.at[0, yh], mys.at[0], myr.at[0], partner))
    go(remote(meta, mc, mus, mur, above))
    for q in range(3):
        across(b0, q, 0)

    panels = a_last, a_mid, a_first
    places = (2, 0), (1, 0), (1, 1), (0, 0)
    holders = section == 3, (section == 1) | (section == 2), section == 0

    def panel(b, s):
        return panels[places[s][0]].at[b, places[s][1]]

    def root_copies(b, g):
        c = b // 2 * 4 + yl * 2 + b % 2
        to = (row_above if g == 0 else row, c)
        return remote(blocks.at[b], panels[g].at[b, section - 1 if g == 1 else 0], rs.at[b], rr.at[section], to)

    def root_lists(d, last):
        s = SECTIONS - 1 if last else section
        return remote(meta, ma.at[s], rms.at[d], rmr.at[s], (row_above if last else row, (col + d) % 16))

    def each_root_copy(act):
        for g in range(3):
            @pl.when(holders[g])
            def _():
                for d in range(0 if g == 0 else 1, SLOTS):
                    act(root_copies((chunk + d) % SLOTS, g))

    def each_root_list(act):
        @pl.when(section < 3)
        def _():
            for d in range(1, 16):
                act(root_lists(d, False))

        @pl.when(section == 3)
        def _():
            for d in range(16):
                act(root_lists(d, True))

    each_root_list(lambda copy: copy.start())
    each_root_copy(lambda copy: copy.start())

    pl.semaphore_wait(ready, 1)
    go(remote(meta, mb.at[1, yh], mzs.at[0], mzr.at[0], below))
    for q in range(SLOTS):
        go(remote(b0.at[yh, q], b1.at[yh, q], zs.at[q], zr.at[q], below))

    for g in (1, 2):
        @pl.when(holders[g])
        def _():
            at = panels[g].at[chunk, section - 1 if g == 1 else 0]
            mine = pltpu.make_async_copy(blocks.at[chunk], at, local_sem.at[3])
            mine.start()
            ma[section] = meta[...]
            mine.wait()

    def from_here(s):
        return ((z + s) % 16 if s < 3 else (z + 2) % 16) // 2 % 2 == yl

    def cross(s):
        return remote(panel(chunk, s), panel(chunk, s), ks.at[s], kr.at[s], opposite)

    def panel_lists(s):
        def arrived():
            remote(meta, ma.at[s], rms.at[0], rmr.at[s], partner).wait_recv()

        if s < 3:
            pl.when(section != s)(arrived)
        else:
            arrived()

    def panel_cross(s):
        @pl.when(from_here(s))
        def _():
            def arrived():
                remote(blocks.at[0], panel(0, s), rs.at[0], rr.at[s], partner).wait_recv()

            if s < 3:
                pl.when(section != s)(arrived)
            else:
                arrived()
            cross(s).start()

    def part(b, g):
        return panels[g].at[b]

    def panel_spread(g):
        for s in ((3,), (1, 2), (0,))[g]:
            @pl.when(jnp.logical_not(from_here(s)))
            def _():
                cross(s).wait_recv()
        for d in range(1, 4):
            go(remote(part(chunk, g), part(chunk, g), gs.at[g, d], gr.at[g, d], line[d - 1]), g)
        go(remote(part(chunk, g), part(chunk, g), cs.at[g, 0], cr.at[g, 0], twin), g)

    def panel_twin(g):
        for d in range(1, 4):
            b = (x + 4 - d) % 4 * 2 + core
            remote(part(b, g), part(b, g), gs.at[g, d], gr.at[g, d], twin).wait_recv()
            go(remote(part(b, g), part(b, g), cs.at[g, d], cr.at[g, d], twin), g)

    def panel_whole(g):
        for d in range(4):
            b = (x + 4 - d) % 4 * 2 + 1 - core
            remote(part(b, g), part(b, g), cs.at[g, d], cr.at[g, d], twin).wait_recv()

    def partner_block(ref, q, first):
        remote(ref.at[other, q], ref.at[other, q], ys.at[first + q], yr.at[first + q], partner).wait_recv()

    def from_both(q):
        return remote(b1.at[other, q], b2.at[other, q], zs.at[24 + q], zr.at[24 + q], below)

    n = SLOTS
    to_scalars = pltpu.make_async_copy(table, table_s, local_sem.at[4])

    def match():
        for i in range(3):
            remote(meta, mb.at[i, other], mys.at[i], myr.at[i], partner).wait_recv()
        remote(meta, mc, mus, mur, above).wait_recv()
        for s in range(SECTIONS):
            panel_lists(s)
        lane = lax.broadcasted_iota(jnp.int32, (n, n), 1)
        diag = lax.broadcasted_iota(jnp.int32, (n, n), 0) == lane

        def upright(values):
            wide = jnp.broadcast_to(values, (n, n))
            return jnp.sum(jnp.where(diag, wide, 0), axis=1, keepdims=True)

        for s, (lists, i) in enumerate(((meta, 0), (meta, 1), (meta, 2), (mc, 2))):
            out_rows, out_cols = upright(lists[0:1, 0:n]), upright(lists[1:2, 0:n])
            a_rows, a_cols = ma[s, 0:1, 0:n], ma[s, 1:2, 0:n]
            same_row = (out_rows == a_rows) & (out_rows >= 0)
            found = jnp.full((n, n), -1, jnp.int32)
            for h in range(2):
                for q in range(n):
                    inner, b_col = mb[i, h, 0:1, q:q + 1], mb[i, h, 1:2, q:q + 1]
                    hit = (a_cols == inner + RB * h) & (out_cols == b_col) & (inner >= 0)
                    found = jnp.where(hit, h * n + q, found)
            found = jnp.where(same_row, found, -1)
            matched = jnp.where(found >= 0, 1, 0)
            rank = jnp.zeros((n, n), jnp.int32)
            for p in range(n - 1):
                rank = rank + jnp.where(lane > p, matched[:, p:p + 1], 0)
            for d in range(DEPTH):
                pick = (matched > 0) & (rank == d)
                a_at = n + jnp.sum(jnp.where(pick, lane - n, 0), axis=1, keepdims=True)
                b_at = jnp.sum(jnp.where(pick, found, 0), axis=1, keepdims=True)
                table[s * n:(s + 1) * n, d:d + 1] = a_at
                table[s * n:(s + 1) * n, DEPTH + d:DEPTH + d + 1] = b_at
        to_scalars.start()

    remote(meta, mb.at[1, yh], mzs.at[0], mzr.at[0], below).wait_recv()
    go(remote(mb.at[1, yh], mb.at[2, yh], mzs.at[1], mzr.at[1], below))
    go(remote(mb.at[1, yh], mb.at[1, yh], mys.at[1], myr.at[1], partner))
    for q in range(SLOTS):
        remote(b0.at[yh, q], b1.at[yh, q], zs.at[q], zr.at[q], below).wait_recv()
        go(remote(b1.at[yh, q], b2.at[yh, q], zs.at[8 + q], zr.at[8 + q], below), 1)
        if q < EARLY:
            across(b1, q, 16)
        if q == 4:
            panel_cross(3)
        elif EARLY <= q < 7:
            across(b0, q + (1 if q < 4 else 0), 0)
    remote(meta, mb.at[2, yh], mzs.at[1], mzr.at[1], below).wait_recv()
    go(remote(mb.at[2, yh], mb.at[2, yh], mys.at[2], myr.at[2], partner))
    panel_spread(0)
    panel_cross(2)
    panel_cross(1)

    for q in range(SLOTS):
        remote(b1.at[yh, q], b2.at[yh, q], zs.at[8 + q], zr.at[8 + q], below).wait_recv()
        if q >= EARLY:
            across(b2, q, 8, 1)
        if q == 0:
            across(b0, 7, 0, 1)
        if q == 2:
            match()
        if q == 3:
            panel_spread(1)
            panel_cross(0)
        if q == 4:
            panel_twin(0)
    for q in range(EARLY):
        partner_block(b1, q, 16)
        go(from_both(q), 1)
    for q in range(EARLY, SLOTS):
        across(b1, q, 16, 2)
    panel_spread(2)
    panel_whole(0)
    to_scalars.wait()

    def halves(v):
        high = v.astype(BF16)
        return high, (v - high.astype(F32)).astype(BF16)

    def product(s, t, b_ref):
        lefts, rights = [], []
        for d in range(DEPTH):
            a = panels[places[s][0]][table_s[s * n + t, d], places[s][1]]
            at = table_s[s * n + t, DEPTH + d]
            b = b_ref[at // n, at % n]
            lefts += halves(a)
            wide = jnp.concatenate(halves(b), axis=1)
            rights += [wide, wide]
        both = jnp.dot(jnp.concatenate(lefts, axis=1), jnp.concatenate(rights, axis=0), preferred_element_type=F32)
        return both[:, :BS] + both[:, BS:]

    def down(t):
        return remote(c_down.at[t], c_in.at[t], zs.at[16 + t], zr.at[16 + t], below)

    def sent(when):
        for copy in sends[when]:
            copy.wait_send()

    each_root_list(lambda copy: copy.wait_send())
    each_root_copy(lambda copy: copy.wait_send())
    sent(0)
    for q in range(EARLY, SLOTS):
        partner_block(b2, q, 8)
    for q in range(EARLY):
        from_both(q).wait_recv()

    def last_section(t, carry):
        c_down[t] = product(3, t, b2)
        down(t).start()
        return carry

    lax.fori_loop(0, SLOTS, last_section, 0)
    panel_twin(1)
    panel_whole(1)

    def section_two(t, carry):
        acc[t] = product(2, t, b2)
        return carry

    lax.fori_loop(0, SLOTS, section_two, 0)
    panel_twin(2)
    panel_whole(2)
    for q in range(SLOTS):
        partner_block(b0, q, 0)

    def section_zero(t, carry):
        acc[t] += product(0, t, b0)
        return carry

    lax.fori_loop(0, SLOTS, section_zero, 0)
    for s in range(SECTIONS):
        @pl.when(from_here(s))
        def _():
            cross(s).wait_send()
    sent(1)
    for q in range(EARLY, SLOTS):
        partner_block(b1, q, 16)

    def section_one(t, carry):
        acc[t] += product(1, t, b1)
        return carry

    lax.fori_loop(0, SLOTS, section_one, 0)

    def result(t):
        return pltpu.make_async_copy(acc.at[t], out.at[t], out_sem.at[t])

    def finish(t, carry):
        down(t).wait_recv()
        acc[t] += c_in[t]
        result(t).start()
        return carry

    lax.fori_loop(0, SLOTS, finish, 0)
    for t in range(SLOTS):
        down(t).wait_send()
    sent(2)
    for t in range(SLOTS):
        result(t).wait()


def body(blocks, block_rows, block_cols):
    dma = pltpu.SemaphoreType.DMA
    hbm = pl.BlockSpec(memory_space=pl.ANY)
    tile = pltpu.VMEM((2, SLOTS, BS, BS), F32)
    lists = (8, BS)
    i32 = jnp.int32
    out = pl.pallas_call(
        kernel,
        out_shape=jax.ShapeDtypeStruct((SLOTS, BS, BS), F32),
        in_specs=[hbm, hbm, hbm],
        out_specs=hbm,
        scratch_shapes=[
            pltpu.VMEM((1, SLOTS), i32), pltpu.VMEM((1, SLOTS), i32),
            pltpu.VMEM(lists, i32), pltpu.VMEM((3, 2, *lists), i32), pltpu.VMEM((SECTIONS, *lists), i32),
            pltpu.VMEM(lists, i32),
            tile, tile, tile,
            *(pltpu.VMEM((SLOTS + 1, m, BS, BS), F32) for m in (1, 2, 1)),
            pltpu.VMEM((SLOTS, BS, BS), F32), pltpu.VMEM((SLOTS, BS, BS), F32), pltpu.VMEM((SLOTS, BS, BS), F32),
            pltpu.VMEM((SECTIONS * SLOTS, BS), i32), pltpu.SMEM((SECTIONS * SLOTS, BS), i32),
            dma((5,)), pltpu.SemaphoreType.REGULAR,
            dma((32,)), dma((32,)), dma((24,)), dma((24,)),
            dma((2,)), dma((2,)), dma((3,)), dma((3,)), dma(()), dma(()),
            dma((SLOTS,)), dma((4,)), dma((16,)), dma((4,)), dma((4,)), dma((4,)),
            dma((3, 4)), dma((3, 4)), dma((3, 4)), dma((3, 4)), dma((SLOTS,)),
        ],
        compiler_params=pltpu.CompilerParams(
            collective_id=0, has_side_effects=True, vmem_limit_bytes=56 * 2**20
        ),
        name="four_sections",
    )(blocks[0, 0], block_rows[0], block_cols[0])
    return out[None, None]


def solution(mesh):
    return jax.shard_map(
        body,
        mesh=mesh,
        in_specs=(P("row", "col", None, None, None), P("row", "col", None), P("row", "col", None)),
        out_specs=P("row", "col", None, None, None),
        check_vma=False,
    )
```

```python
import jax
import jax.numpy as jnp
from jax import lax
from jax.experimental import pallas as pl
from jax.experimental.pallas import tpu as pltpu
from jax.sharding import PartitionSpec as P

MESH = pl.DeviceIdType.MESH
BS = 128
SLOTS = 8
RB = 16
SECTIONS = 4
DEPTH = 4
EARLY = 2
F32 = jnp.float32
BF16 = jnp.bfloat16


def kernel(blocks, rows, cols, out, rows_v, cols_v, meta, mb, ma, mc, b0, b1, b2, a_last, a_mid, a_first, c_down, c_in, acc,
           table, table_s, local_sem, ready, zs, zr, ys, yr, mzs, mzr, mys, myr, mus, mur,
           rs, rr, rms, rmr, ks, kr, gs, gr, cs, cr, out_sem):
    row, col = lax.axis_index("row"), lax.axis_index("col")
    z, yh = row // 2, row % 2
    other = 1 - yh
    x, yl, core = col // 4, (col // 2) % 2, col % 2
    row_below, row_above = (z + 15) % 16 * 2 + yh, (z + 1) % 16 * 2 + yh
    below, above = (row_below, col), (row_above, col)
    partner = (z * 2 + other, col)
    twin = (row, x * 4 + yl * 2 + 1 - core)
    opposite = (row, x * 4 + (1 - yl) * 2 + core)
    section = (col + 16 - z) % 16
    chunk = x * 2 + core
    line = [(row, (x + d) % 4 * 4 + yl * 2 + core) for d in range(1, 4)]

    def remote(src, dst, send, recv, to):
        return pltpu.make_async_remote_copy(
            src_ref=src, dst_ref=dst, send_sem=send, recv_sem=recv, device_id=to, device_id_type=MESH
        )

    def signal(sem, to):
        pl.semaphore_signal(sem, inc=1, device_id=to, device_id_type=MESH)

    barrier = pltpu.get_barrier_semaphore()
    for to in (below, partner, twin, opposite, *line):
        signal(barrier, to)
    for s in range(3):
        @pl.when(section != s)
        def _():
            signal(barrier, (row, (z + s) % 16))
    signal(barrier, (row_below, (z + 2) % 16))

    own = pltpu.make_async_copy(blocks, b0.at[yh], local_sem.at[0])
    own.start()
    own_rows = pltpu.make_async_copy(rows, rows_v, local_sem.at[1])
    own_rows.start()
    own_cols = pltpu.make_async_copy(cols, cols_v, local_sem.at[2])
    own_cols.start()
    for ref in (a_last, a_mid, a_first):
        ref[SLOTS] = jnp.zeros(ref.shape[1:], F32)
    meta[...] = jnp.full((8, BS), -1, jnp.int32)
    own_rows.wait()
    own_cols.wait()
    meta[0:1, 0:SLOTS] = rows_v[...]
    meta[1:2, 0:SLOTS] = cols_v[...]
    mb[0, yh] = meta[...]
    own.wait()

    pl.semaphore_wait(barrier, 7 + jnp.where(section < 3, 15, jnp.where(section == 3, 16, 0)))
    signal(ready, above)

    sends = [], [], []

    def go(copy, when=0):
        copy.start()
        sends[when].append(copy)

    def across(ref, q, first, when=0):
        go(remote(ref.at[yh, q], ref.at[yh, q], ys.at[first + q], yr.at[first + q], partner), when)

    go(remote(meta, mb.at[0, yh], mys.at[0], myr.at[0], partner))
    go(remote(meta, mc, mus, mur, above))
    for q in range(3):
        across(b0, q, 0)

    panels = a_last, a_mid, a_first
    places = (2, 0), (1, 0), (1, 1), (0, 0)
    holders = section == 3, (section == 1) | (section == 2), section == 0

    def panel(b, s):
        return panels[places[s][0]].at[b, places[s][1]]

    def root_copies(b, g):
        c = b // 2 * 4 + yl * 2 + b % 2
        to = (row_above if g == 0 else row, c)
        return remote(blocks.at[b], panels[g].at[b, section - 1 if g == 1 else 0], rs.at[b], rr.at[section], to)

    def root_lists(d, last):
        s = SECTIONS - 1 if last else section
        return remote(meta, ma.at[s], rms.at[d], rmr.at[s], (row_above if last else row, (col + d) % 16))

    def each_root_copy(act):
        for g in range(3):
            @pl.when(holders[g])
            def _():
                for d in range(0 if g == 0 else 1, SLOTS):
                    act(root_copies((chunk + d) % SLOTS, g))

    def each_root_list(act):
        @pl.when(section < 3)
        def _():
            for d in range(1, 16):
                act(root_lists(d, False))

        @pl.when(section == 3)
        def _():
            for d in range(16):
                act(root_lists(d, True))

    each_root_list(lambda copy: copy.start())
    each_root_copy(lambda copy: copy.start())

    pl.semaphore_wait(ready, 1)
    go(remote(meta, mb.at[1, yh], mzs.at[0], mzr.at[0], below))
    for q in range(SLOTS):
        go(remote(b0.at[yh, q], b1.at[yh, q], zs.at[q], zr.at[q], below))

    for g in (1, 2):
        @pl.when(holders[g])
        def _():
            at = panels[g].at[chunk, section - 1 if g == 1 else 0]
            mine = pltpu.make_async_copy(blocks.at[chunk], at, local_sem.at[3])
            mine.start()
            ma[section] = meta[...]
            mine.wait()

    def from_here(s):
        return ((z + s) % 16 if s < 3 else (z + 2) % 16) // 2 % 2 == yl

    def cross(s):
        return remote(panel(chunk, s), panel(chunk, s), ks.at[s], kr.at[s], opposite)

    def panel_lists(s):
        def arrived():
            remote(meta, ma.at[s], rms.at[0], rmr.at[s], partner).wait_recv()

        if s < 3:
            pl.when(section != s)(arrived)
        else:
            arrived()

    def panel_cross(s):
        @pl.when(from_here(s))
        def _():
            def arrived():
                remote(blocks.at[0], panel(0, s), rs.at[0], rr.at[s], partner).wait_recv()

            if s < 3:
                pl.when(section != s)(arrived)
            else:
                arrived()
            cross(s).start()

    def part(b, g):
        return panels[g].at[b]

    def panel_spread(g):
        for s in ((3,), (1, 2), (0,))[g]:
            @pl.when(jnp.logical_not(from_here(s)))
            def _():
                cross(s).wait_recv()
        for d in range(1, 4):
            go(remote(part(chunk, g), part(chunk, g), gs.at[g, d], gr.at[g, d], line[d - 1]), g)
        go(remote(part(chunk, g), part(chunk, g), cs.at[g, 0], cr.at[g, 0], twin), g)

    def panel_twin(g):
        for d in range(1, 4):
            b = (x + 4 - d) % 4 * 2 + core
            remote(part(b, g), part(b, g), gs.at[g, d], gr.at[g, d], twin).wait_recv()
            go(remote(part(b, g), part(b, g), cs.at[g, d], cr.at[g, d], twin), g)

    def panel_whole(g):
        for d in range(4):
            b = (x + 4 - d) % 4 * 2 + 1 - core
            remote(part(b, g), part(b, g), cs.at[g, d], cr.at[g, d], twin).wait_recv()

    def partner_block(ref, q, first):
        remote(ref.at[other, q], ref.at[other, q], ys.at[first + q], yr.at[first + q], partner).wait_recv()

    def from_both(q):
        return remote(b1.at[other, q], b2.at[other, q], zs.at[24 + q], zr.at[24 + q], below)

    n = SLOTS
    to_scalars = pltpu.make_async_copy(table, table_s, local_sem.at[4])

    def match():
        for i in range(3):
            remote(meta, mb.at[i, other], mys.at[i], myr.at[i], partner).wait_recv()
        remote(meta, mc, mus, mur, above).wait_recv()
        for s in range(SECTIONS):
            panel_lists(s)
        lane = lax.broadcasted_iota(jnp.int32, (n, n), 1)
        diag = lax.broadcasted_iota(jnp.int32, (n, n), 0) == lane

        def upright(values):
            wide = jnp.broadcast_to(values, (n, n))
            return jnp.sum(jnp.where(diag, wide, 0), axis=1, keepdims=True)

        for s, (lists, i) in enumerate(((meta, 0), (meta, 1), (meta, 2), (mc, 2))):
            out_rows, out_cols = upright(lists[0:1, 0:n]), upright(lists[1:2, 0:n])
            a_rows, a_cols = ma[s, 0:1, 0:n], ma[s, 1:2, 0:n]
            same_row = (out_rows == a_rows) & (out_rows >= 0)
            found = jnp.full((n, n), -1, jnp.int32)
            for h in range(2):
                for q in range(n):
                    inner, b_col = mb[i, h, 0:1, q:q + 1], mb[i, h, 1:2, q:q + 1]
                    hit = (a_cols == inner + RB * h) & (out_cols == b_col) & (inner >= 0)
                    found = jnp.where(hit, h * n + q, found)
            found = jnp.where(same_row, found, -1)
            matched = jnp.where(found >= 0, 1, 0)
            rank = jnp.zeros((n, n), jnp.int32)
            for p in range(n - 1):
                rank = rank + jnp.where(lane > p, matched[:, p:p + 1], 0)
            for d in range(DEPTH):
                pick = (matched > 0) & (rank == d)
                a_at = n + jnp.sum(jnp.where(pick, lane - n, 0), axis=1, keepdims=True)
                b_at = jnp.sum(jnp.where(pick, found, 0), axis=1, keepdims=True)
                table[s * n:(s + 1) * n, d:d + 1] = a_at
                table[s * n:(s + 1) * n, DEPTH + d:DEPTH + d + 1] = b_at
        to_scalars.start()

    remote(meta, mb.at[1, yh], mzs.at[0], mzr.at[0], below).wait_recv()
    go(remote(mb.at[1, yh], mb.at[2, yh], mzs.at[1], mzr.at[1], below))
    go(remote(mb.at[1, yh], mb.at[1, yh], mys.at[1], myr.at[1], partner))
    for q in range(SLOTS):
        remote(b0.at[yh, q], b1.at[yh, q], zs.at[q], zr.at[q], below).wait_recv()
        go(remote(b1.at[yh, q], b2.at[yh, q], zs.at[8 + q], zr.at[8 + q], below), 1)
        if q < EARLY:
            across(b1, q, 16)
        if q == 6:
            panel_cross(3)
        elif EARLY <= q:
            across(b0, q + (1 if q < 6 else 0), 0)
    remote(meta, mb.at[2, yh], mzs.at[1], mzr.at[1], below).wait_recv()
    go(remote(mb.at[2, yh], mb.at[2, yh], mys.at[2], myr.at[2], partner))
    panel_cross(2)
    panel_cross(1)

    for q in range(SLOTS):
        remote(b1.at[yh, q], b2.at[yh, q], zs.at[8 + q], zr.at[8 + q], below).wait_recv()
        if q >= EARLY:
            across(b2, q, 8, 1)
        if q == 2:
            match()
        if q == 3:
            panel_spread(0)
        if q == 4:
            panel_spread(1)
            panel_cross(0)
    for q in range(EARLY):
        partner_block(b1, q, 16)
        go(from_both(q), 1)
    for q in range(EARLY, SLOTS):
        across(b1, q, 16, 2)
    panel_spread(2)
    panel_twin(0)
    panel_whole(0)
    to_scalars.wait()

    def halves(v):
        high = v.astype(BF16)
        return high, (v - high.astype(F32)).astype(BF16)

    def product(s, t, b_ref):
        lefts, rights = [], []
        for d in range(DEPTH):
            a = panels[places[s][0]][table_s[s * n + t, d], places[s][1]]
            at = table_s[s * n + t, DEPTH + d]
            b = b_ref[at // n, at % n]
            lefts += halves(a)
            wide = jnp.concatenate(halves(b), axis=1)
            rights += [wide, wide]
        both = jnp.dot(jnp.concatenate(lefts, axis=1), jnp.concatenate(rights, axis=0), preferred_element_type=F32)
        return both[:, :BS] + both[:, BS:]

    def down(t):
        return remote(c_down.at[t], c_in.at[t], zs.at[16 + t], zr.at[16 + t], below)

    def sent(when):
        for copy in sends[when]:
            copy.wait_send()

    each_root_list(lambda copy: copy.wait_send())
    each_root_copy(lambda copy: copy.wait_send())
    sent(0)
    for q in range(EARLY, SLOTS):
        partner_block(b2, q, 8)
    for q in range(EARLY):
        from_both(q).wait_recv()

    def last_section(i, carry):
        c_down[2 * i], c_down[2 * i + 1] = product(3, 2 * i, b2), product(3, 2 * i + 1, b2)
        down(2 * i).start()
        down(2 * i + 1).start()
        return carry

    lax.fori_loop(0, SLOTS // 2, last_section, 0)
    panel_twin(1)
    panel_whole(1)

    def section_two(i, carry):
        acc[2 * i], acc[2 * i + 1] = product(2, 2 * i, b2), product(2, 2 * i + 1, b2)
        return carry

    lax.fori_loop(0, SLOTS // 2, section_two, 0)
    panel_twin(2)
    panel_whole(2)
    for q in range(SLOTS):
        partner_block(b0, q, 0)

    for s in range(SECTIONS):
        @pl.when(from_here(s))
        def _():
            cross(s).wait_send()
    sent(1)
    for q in range(EARLY, SLOTS):
        partner_block(b1, q, 16)

    def sections_zero_one(t, carry):
        acc[t] += product(0, t, b0) + product(1, t, b1)
        return carry

    lax.fori_loop(0, SLOTS, sections_zero_one, 0)

    def result(t):
        return pltpu.make_async_copy(acc.at[t], out.at[t], out_sem.at[t])

    def finish(t, carry):
        down(t).wait_recv()
        acc[t] += c_in[t]
        result(t).start()
        return carry

    lax.fori_loop(0, SLOTS, finish, 0)
    for t in range(SLOTS):
        down(t).wait_send()
    sent(2)
    for t in range(SLOTS):
        result(t).wait()


def body(blocks, block_rows, block_cols):
    dma = pltpu.SemaphoreType.DMA
    hbm = pl.BlockSpec(memory_space=pl.ANY)
    tile = pltpu.VMEM((2, SLOTS, BS, BS), F32)
    lists = (8, BS)
    i32 = jnp.int32
    out = pl.pallas_call(
        kernel,
        out_shape=jax.ShapeDtypeStruct((SLOTS, BS, BS), F32),
        in_specs=[hbm, hbm, hbm],
        out_specs=hbm,
        scratch_shapes=[
            pltpu.VMEM((1, SLOTS), i32), pltpu.VMEM((1, SLOTS), i32),
            pltpu.VMEM(lists, i32), pltpu.VMEM((3, 2, *lists), i32), pltpu.VMEM((SECTIONS, *lists), i32),
            pltpu.VMEM(lists, i32),
            tile, tile, tile,
            *(pltpu.VMEM((SLOTS + 1, m, BS, BS), F32) for m in (1, 2, 1)),
            pltpu.VMEM((SLOTS, BS, BS), F32), pltpu.VMEM((SLOTS, BS, BS), F32), pltpu.VMEM((SLOTS, BS, BS), F32),
            pltpu.VMEM((SECTIONS * SLOTS, BS), i32), pltpu.SMEM((SECTIONS * SLOTS, BS), i32),
            dma((5,)), pltpu.SemaphoreType.REGULAR,
            dma((32,)), dma((32,)), dma((24,)), dma((24,)),
            dma((2,)), dma((2,)), dma((3,)), dma((3,)), dma(()), dma(()),
            dma((SLOTS,)), dma((4,)), dma((16,)), dma((4,)), dma((4,)), dma((4,)),
            dma((3, 4)), dma((3, 4)), dma((3, 4)), dma((3, 4)), dma((SLOTS,)),
        ],
        compiler_params=pltpu.CompilerParams(
            collective_id=0, has_side_effects=True, vmem_limit_bytes=53 * 2**20
        ),
        name="four_sections",
    )(blocks[0, 0], block_rows[0], block_cols[0])
    return out[None, None]


def solution(mesh):
    return jax.shard_map(
        body,
        mesh=mesh,
        in_specs=(P("row", "col", None, None, None), P("row", "col", None), P("row", "col", None)),
        out_specs=P("row", "col", None, None, None),
        check_vma=False,
    )
```

```python
import jax
import jax.numpy as jnp
from jax import lax
from jax.experimental import pallas as pl
from jax.experimental.pallas import tpu as pltpu
from jax.sharding import PartitionSpec as P

MESH = pl.DeviceIdType.MESH
BS = 128
SLOTS = 8
RB = 16
SECTIONS = 4
DEPTH = 4
EARLY = 2
F32 = jnp.float32
BF16 = jnp.bfloat16


def kernel(blocks, rows, cols, out, rows_v, cols_v, meta, mb, ma, mc, b0, b1, b2, a_last, a_mid, a_first, c_down, c_in, acc,
           table, table_s, local_sem, ready, zs, zr, ys, yr, mzs, mzr, mys, myr, mus, mur,
           rs, rr, rms, rmr, ks, kr, gs, gr, cs, cr, out_sem):
    row, col = lax.axis_index("row"), lax.axis_index("col")
    z, yh = row // 2, row % 2
    other = 1 - yh
    x, yl, core = col // 4, (col // 2) % 2, col % 2
    row_below, row_above = (z + 15) % 16 * 2 + yh, (z + 1) % 16 * 2 + yh
    below, above = (row_below, col), (row_above, col)
    partner = (z * 2 + other, col)
    twin = (row, x * 4 + yl * 2 + 1 - core)
    opposite = (row, x * 4 + (1 - yl) * 2 + core)
    section = (col + 16 - z) % 16
    chunk = x * 2 + core
    line = [(row, (x + d) % 4 * 4 + yl * 2 + core) for d in range(1, 4)]

    def remote(src, dst, send, recv, to):
        return pltpu.make_async_remote_copy(
            src_ref=src, dst_ref=dst, send_sem=send, recv_sem=recv, device_id=to, device_id_type=MESH
        )

    def signal(sem, to):
        pl.semaphore_signal(sem, inc=1, device_id=to, device_id_type=MESH)

    barrier = pltpu.get_barrier_semaphore()
    for to in (below, partner, twin, opposite, *line):
        signal(barrier, to)
    for s in range(3):
        @pl.when(section != s)
        def _():
            signal(barrier, (row, (z + s) % 16))
    signal(barrier, (row_below, (z + 2) % 16))

    own = pltpu.make_async_copy(blocks, b0.at[yh], local_sem.at[0])
    own.start()
    own_rows = pltpu.make_async_copy(rows, rows_v, local_sem.at[1])
    own_rows.start()
    own_cols = pltpu.make_async_copy(cols, cols_v, local_sem.at[2])
    own_cols.start()
    for ref in (a_last, a_mid, a_first):
        ref[SLOTS] = jnp.zeros(ref.shape[1:], F32)
    meta[...] = jnp.full((8, BS), -1, jnp.int32)
    own_rows.wait()
    own_cols.wait()
    meta[0:1, 0:SLOTS] = rows_v[...]
    meta[1:2, 0:SLOTS] = cols_v[...]
    mb[0, yh] = meta[...]
    own.wait()

    pl.semaphore_wait(barrier, 7 + jnp.where(section < 3, 15, jnp.where(section == 3, 16, 0)))
    signal(ready, above)

    sends = [], [], []

    def go(copy, when=0):
        copy.start()
        sends[when].append(copy)

    def across(ref, q, first, when=0):
        go(remote(ref.at[yh, q], ref.at[yh, q], ys.at[first + q], yr.at[first + q], partner), when)

    go(remote(meta, mb.at[0, yh], mys.at[0], myr.at[0], partner))
    go(remote(meta, mc, mus, mur, above))
    for q in range(3):
        across(b0, q, 0)

    panels = a_last, a_mid, a_first
    places = (2, 0), (1, 0), (1, 1), (0, 0)
    holders = section == 3, (section == 1) | (section == 2), section == 0

    def panel(b, s):
        return panels[places[s][0]].at[b, places[s][1]]

    def root_copies(b, g):
        c = b // 2 * 4 + yl * 2 + b % 2
        to = (row_above if g == 0 else row, c)
        return remote(blocks.at[b], panels[g].at[b, section - 1 if g == 1 else 0], rs.at[b], rr.at[section], to)

    def root_lists(d, last):
        s = SECTIONS - 1 if last else section
        return remote(meta, ma.at[s], rms.at[d], rmr.at[s], (row_above if last else row, (col + d) % 16))

    def each_root_copy(act):
        for g in range(3):
            @pl.when(holders[g])
            def _():
                for d in range(0 if g == 0 else 1, SLOTS):
                    act(root_copies((chunk + d) % SLOTS, g))

    def each_root_list(act):
        @pl.when(section < 3)
        def _():
            for d in range(1, 16):
                act(root_lists(d, False))

        @pl.when(section == 3)
        def _():
            for d in range(16):
                act(root_lists(d, True))

    each_root_list(lambda copy: copy.start())
    each_root_copy(lambda copy: copy.start())

    pl.semaphore_wait(ready, 1)
    go(remote(meta, mb.at[1, yh], mzs.at[0], mzr.at[0], below))
    for q in range(SLOTS):
        go(remote(b0.at[yh, q], b1.at[yh, q], zs.at[q], zr.at[q], below))

    for g in (1, 2):
        @pl.when(holders[g])
        def _():
            at = panels[g].at[chunk, section - 1 if g == 1 else 0]
            mine = pltpu.make_async_copy(blocks.at[chunk], at, local_sem.at[3])
            mine.start()
            ma[section] = meta[...]
            mine.wait()

    def from_here(s):
        return ((z + s) % 16 if s < 3 else (z + 2) % 16) // 2 % 2 == yl

    def cross(s):
        return remote(panel(chunk, s), panel(chunk, s), ks.at[s], kr.at[s], opposite)

    def panel_lists(s):
        def arrived():
            remote(meta, ma.at[s], rms.at[0], rmr.at[s], partner).wait_recv()

        if s < 3:
            pl.when(section != s)(arrived)
        else:
            arrived()

    def panel_cross(s):
        @pl.when(from_here(s))
        def _():
            def arrived():
                remote(blocks.at[0], panel(0, s), rs.at[0], rr.at[s], partner).wait_recv()

            if s < 3:
                pl.when(section != s)(arrived)
            else:
                arrived()
            cross(s).start()

    def part(b, g):
        return panels[g].at[b]

    def panel_spread(g):
        for s in ((3,), (1, 2), (0,))[g]:
            @pl.when(jnp.logical_not(from_here(s)))
            def _():
                cross(s).wait_recv()
        for d in range(1, 4):
            go(remote(part(chunk, g), part(chunk, g), gs.at[g, d], gr.at[g, d], line[d - 1]), g)
        go(remote(part(chunk, g), part(chunk, g), cs.at[g, 0], cr.at[g, 0], twin), g)

    def panel_twin(g):
        for d in range(1, 4):
            b = (x + 4 - d) % 4 * 2 + core
            remote(part(b, g), part(b, g), gs.at[g, d], gr.at[g, d], twin).wait_recv()
            go(remote(part(b, g), part(b, g), cs.at[g, d], cr.at[g, d], twin), g)

    def panel_whole(g):
        for d in range(4):
            b = (x + 4 - d) % 4 * 2 + 1 - core
            remote(part(b, g), part(b, g), cs.at[g, d], cr.at[g, d], twin).wait_recv()

    def partner_block(ref, q, first):
        remote(ref.at[other, q], ref.at[other, q], ys.at[first + q], yr.at[first + q], partner).wait_recv()

    def from_both(q):
        return remote(b1.at[other, q], b2.at[other, q], zs.at[24 + q], zr.at[24 + q], below)

    n = SLOTS
    to_scalars = pltpu.make_async_copy(table, table_s, local_sem.at[4])

    def match():
        for i in range(3):
            remote(meta, mb.at[i, other], mys.at[i], myr.at[i], partner).wait_recv()
        remote(meta, mc, mus, mur, above).wait_recv()
        for s in range(SECTIONS):
            panel_lists(s)
        lane = lax.broadcasted_iota(jnp.int32, (n, n), 1)
        diag = lax.broadcasted_iota(jnp.int32, (n, n), 0) == lane

        def upright(values):
            wide = jnp.broadcast_to(values, (n, n))
            return jnp.sum(jnp.where(diag, wide, 0), axis=1, keepdims=True)

        for s, (lists, i) in enumerate(((meta, 0), (meta, 1), (meta, 2), (mc, 2))):
            out_rows, out_cols = upright(lists[0:1, 0:n]), upright(lists[1:2, 0:n])
            a_rows, a_cols = ma[s, 0:1, 0:n], ma[s, 1:2, 0:n]
            same_row = (out_rows == a_rows) & (out_rows >= 0)
            found = jnp.full((n, n), -1, jnp.int32)
            for h in range(2):
                for q in range(n):
                    inner, b_col = mb[i, h, 0:1, q:q + 1], mb[i, h, 1:2, q:q + 1]
                    hit = (a_cols == inner + RB * h) & (out_cols == b_col) & (inner >= 0)
                    found = jnp.where(hit, h * n + q, found)
            found = jnp.where(same_row, found, -1)
            matched = jnp.where(found >= 0, 1, 0)
            rank = jnp.zeros((n, n), jnp.int32)
            for p in range(n - 1):
                rank = rank + jnp.where(lane > p, matched[:, p:p + 1], 0)
            for d in range(DEPTH):
                pick = (matched > 0) & (rank == d)
                a_at = n + jnp.sum(jnp.where(pick, lane - n, 0), axis=1, keepdims=True)
                b_at = jnp.sum(jnp.where(pick, found, 0), axis=1, keepdims=True)
                table[s * n:(s + 1) * n, d:d + 1] = a_at
                table[s * n:(s + 1) * n, DEPTH + d:DEPTH + d + 1] = b_at
        to_scalars.start()

    remote(meta, mb.at[1, yh], mzs.at[0], mzr.at[0], below).wait_recv()
    go(remote(mb.at[1, yh], mb.at[2, yh], mzs.at[1], mzr.at[1], below))
    go(remote(mb.at[1, yh], mb.at[1, yh], mys.at[1], myr.at[1], partner))
    for q in range(SLOTS):
        remote(b0.at[yh, q], b1.at[yh, q], zs.at[q], zr.at[q], below).wait_recv()
        go(remote(b1.at[yh, q], b2.at[yh, q], zs.at[8 + q], zr.at[8 + q], below), 1)
        if q < EARLY:
            across(b1, q, 16)
        if q == 6:
            panel_cross(3)
        elif EARLY <= q < EARLY + 4:
            across(b0, q + 1, 0)
    remote(meta, mb.at[2, yh], mzs.at[1], mzr.at[1], below).wait_recv()
    go(remote(mb.at[2, yh], mb.at[2, yh], mys.at[2], myr.at[2], partner))
    panel_cross(2)
    panel_cross(1)

    for q in range(SLOTS):
        remote(b1.at[yh, q], b2.at[yh, q], zs.at[8 + q], zr.at[8 + q], below).wait_recv()
        if q >= EARLY:
            across(b2, q, 8, 1)
        if q == 2:
            match()
        if q == 3:
            panel_spread(0)
        if q == 4:
            panel_spread(1)
            panel_cross(0)
    for q in range(EARLY):
        partner_block(b1, q, 16)
        go(from_both(q), 1)
    for q in range(EARLY, SLOTS):
        across(b1, q, 16, 2)
    across(b0, SLOTS - 1, 0, 2)
    panel_spread(2)
    panel_twin(0)
    panel_whole(0)
    to_scalars.wait()

    def halves(v):
        high = v.astype(BF16)
        return high, (v - high.astype(F32)).astype(BF16)

    def product(s, t, b_ref):
        lefts, rights = [], []
        for d in range(DEPTH):
            a = panels[places[s][0]][table_s[s * n + t, d], places[s][1]]
            at = table_s[s * n + t, DEPTH + d]
            b = b_ref[at // n, at % n]
            lefts += halves(a)
            wide = jnp.concatenate(halves(b), axis=1)
            rights += [wide, wide]
        both = jnp.dot(jnp.concatenate(lefts, axis=1), jnp.concatenate(rights, axis=0), preferred_element_type=F32)
        return both[:, :BS] + both[:, BS:]

    def down(t):
        return remote(c_down.at[t], c_in.at[t], zs.at[16 + t], zr.at[16 + t], below)

    def sent(when):
        for copy in sends[when]:
            copy.wait_send()

    each_root_list(lambda copy: copy.wait_send())
    each_root_copy(lambda copy: copy.wait_send())
    sent(0)
    for q in range(EARLY, SLOTS):
        partner_block(b2, q, 8)
    for q in range(EARLY):
        from_both(q).wait_recv()

    def last_section(i, carry):
        c_down[2 * i], c_down[2 * i + 1] = product(3, 2 * i, b2), product(3, 2 * i + 1, b2)
        down(2 * i).start()
        down(2 * i + 1).start()
        return carry

    lax.fori_loop(0, SLOTS // 2, last_section, 0)
    panel_twin(1)
    panel_whole(1)

    def section_two(i, carry):
        acc[2 * i], acc[2 * i + 1] = product(2, 2 * i, b2), product(2, 2 * i + 1, b2)
        return carry

    lax.fori_loop(0, SLOTS // 2, section_two, 0)
    panel_twin(2)
    panel_whole(2)
    for q in range(SLOTS):
        partner_block(b0, q, 0)

    for s in range(SECTIONS):
        @pl.when(from_here(s))
        def _():
            cross(s).wait_send()
    sent(1)
    for q in range(EARLY, SLOTS):
        partner_block(b1, q, 16)

    def sections_zero_one(i, carry):
        first, second = 2 * i, 2 * i + 1
        acc[first], acc[second] = (
            acc[first] + product(0, first, b0) + product(1, first, b1),
            acc[second] + product(0, second, b0) + product(1, second, b1),
        )
        return carry

    lax.fori_loop(0, SLOTS // 2, sections_zero_one, 0)

    def result(t):
        return pltpu.make_async_copy(acc.at[t], out.at[t], out_sem.at[t])

    def finish(t, carry):
        down(t).wait_recv()
        acc[t] += c_in[t]
        result(t).start()
        return carry

    lax.fori_loop(0, SLOTS, finish, 0)
    for t in range(SLOTS):
        down(t).wait_send()
    sent(2)
    for t in range(SLOTS):
        result(t).wait()


def body(blocks, block_rows, block_cols):
    dma = pltpu.SemaphoreType.DMA
    hbm = pl.BlockSpec(memory_space=pl.ANY)
    tile = pltpu.VMEM((2, SLOTS, BS, BS), F32)
    lists = (8, BS)
    i32 = jnp.int32
    out = pl.pallas_call(
        kernel,
        out_shape=jax.ShapeDtypeStruct((SLOTS, BS, BS), F32),
        in_specs=[hbm, hbm, hbm],
        out_specs=hbm,
        scratch_shapes=[
            pltpu.VMEM((1, SLOTS), i32), pltpu.VMEM((1, SLOTS), i32),
            pltpu.VMEM(lists, i32), pltpu.VMEM((3, 2, *lists), i32), pltpu.VMEM((SECTIONS, *lists), i32),
            pltpu.VMEM(lists, i32),
            tile, tile, tile,
            *(pltpu.VMEM((SLOTS + 1, m, BS, BS), F32) for m in (1, 2, 1)),
            pltpu.VMEM((SLOTS, BS, BS), F32), pltpu.VMEM((SLOTS, BS, BS), F32), pltpu.VMEM((SLOTS, BS, BS), F32),
            pltpu.VMEM((SECTIONS * SLOTS, BS), i32), pltpu.SMEM((SECTIONS * SLOTS, BS), i32),
            dma((5,)), pltpu.SemaphoreType.REGULAR,
            dma((32,)), dma((32,)), dma((24,)), dma((24,)),
            dma((2,)), dma((2,)), dma((3,)), dma((3,)), dma(()), dma(()),
            dma((SLOTS,)), dma((4,)), dma((16,)), dma((4,)), dma((4,)), dma((4,)),
            dma((3, 4)), dma((3, 4)), dma((3, 4)), dma((3, 4)), dma((SLOTS,)),
        ],
        compiler_params=pltpu.CompilerParams(
            collective_id=0, has_side_effects=True, vmem_limit_bytes=53 * 2**20
        ),
        name="four_sections",
    )(blocks[0, 0], block_rows[0], block_cols[0])
    return out[None, None]


def solution(mesh):
    return jax.shard_map(
        body,
        mesh=mesh,
        in_specs=(P("row", "col", None, None, None), P("row", "col", None), P("row", "col", None)),
        out_specs=P("row", "col", None, None, None),
        check_vma=False,
    )
```

```python
import jax
import jax.numpy as jnp
from jax import lax
from jax.experimental import pallas as pl
from jax.experimental.pallas import tpu as pltpu
from jax.sharding import PartitionSpec as P

MESH = pl.DeviceIdType.MESH
BS = 128
SLOTS = 8
RB = 16
SECTIONS = 4
DEPTH = 4
EARLY = 2
F32 = jnp.float32
BF16 = jnp.bfloat16


def kernel(blocks, rows, cols, out, rows_v, cols_v, meta, mb, ma, mc, b0, b1, b2, a_last, a_mid, a_first, c_down, c_in, acc,
           table, table_s, local_sem, ready, zs, zr, ys, yr, mzs, mzr, mys, myr, mus, mur,
           rs, rr, rms, rmr, ks, kr, gs, gr, cs, cr, out_sem):
    row, col = lax.axis_index("row"), lax.axis_index("col")
    z, yh = row // 2, row % 2
    other = 1 - yh
    x, yl, core = col // 4, (col // 2) % 2, col % 2
    row_below, row_above = (z + 15) % 16 * 2 + yh, (z + 1) % 16 * 2 + yh
    below, above = (row_below, col), (row_above, col)
    partner = (z * 2 + other, col)
    twin = (row, x * 4 + yl * 2 + 1 - core)
    opposite = (row, x * 4 + (1 - yl) * 2 + core)
    section = (col + 16 - z) % 16
    chunk = x * 2 + core
    line = [(row, (x + d) % 4 * 4 + yl * 2 + core) for d in range(1, 4)]

    def remote(src, dst, send, recv, to):
        return pltpu.make_async_remote_copy(
            src_ref=src, dst_ref=dst, send_sem=send, recv_sem=recv, device_id=to, device_id_type=MESH
        )

    def signal(sem, to):
        pl.semaphore_signal(sem, inc=1, device_id=to, device_id_type=MESH)

    barrier = pltpu.get_barrier_semaphore()
    for to in (below, partner, twin, opposite, *line):
        signal(barrier, to)
    for s in range(3):
        @pl.when(section != s)
        def _():
            signal(barrier, (row, (z + s) % 16))
    signal(barrier, (row_below, (z + 2) % 16))

    own = pltpu.make_async_copy(blocks, b0.at[yh], local_sem.at[0])
    own.start()
    own_rows = pltpu.make_async_copy(rows, rows_v, local_sem.at[1])
    own_rows.start()
    own_cols = pltpu.make_async_copy(cols, cols_v, local_sem.at[2])
    own_cols.start()
    for ref in (a_last, a_mid, a_first):
        ref[SLOTS] = jnp.zeros(ref.shape[1:], F32)
    meta[...] = jnp.full((8, BS), -1, jnp.int32)
    own_rows.wait()
    own_cols.wait()
    meta[0:1, 0:SLOTS] = rows_v[...]
    meta[1:2, 0:SLOTS] = cols_v[...]
    mb[0, yh] = meta[...]
    own.wait()

    pl.semaphore_wait(barrier, 7 + jnp.where(section < 3, 15, jnp.where(section == 3, 16, 0)))
    signal(ready, above)

    sends = [], [], []

    def go(copy, when=0):
        copy.start()
        sends[when].append(copy)

    def across(ref, q, first, when=0):
        go(remote(ref.at[yh, q], ref.at[yh, q], ys.at[first + q], yr.at[first + q], partner), when)

    go(remote(meta, mb.at[0, yh], mys.at[0], myr.at[0], partner))
    go(remote(meta, mc, mus, mur, above))
    for q in range(3):
        across(b0, q, 0)

    panels = a_last, a_mid, a_first
    places = (2, 0), (1, 0), (1, 1), (0, 0)
    holders = section == 3, (section == 1) | (section == 2), section == 0

    def panel(b, s):
        return panels[places[s][0]].at[b, places[s][1]]

    def root_copies(b, g):
        c = b // 2 * 4 + yl * 2 + b % 2
        to = (row_above if g == 0 else row, c)
        return remote(blocks.at[b], panels[g].at[b, section - 1 if g == 1 else 0], rs.at[b], rr.at[section], to)

    def root_lists(d, last):
        s = SECTIONS - 1 if last else section
        return remote(meta, ma.at[s], rms.at[d], rmr.at[s], (row_above if last else row, (col + d) % 16))

    def each_root_copy(act):
        for g in range(3):
            @pl.when(holders[g])
            def _():
                for d in range(0 if g == 0 else 1, SLOTS):
                    act(root_copies((chunk + d) % SLOTS, g))

    def each_root_list(act):
        @pl.when(section < 3)
        def _():
            for d in range(1, 16):
                act(root_lists(d, False))

        @pl.when(section == 3)
        def _():
            for d in range(16):
                act(root_lists(d, True))

    each_root_list(lambda copy: copy.start())
    each_root_copy(lambda copy: copy.start())

    pl.semaphore_wait(ready, 1)
    go(remote(meta, mb.at[1, yh], mzs.at[0], mzr.at[0], below))
    for q in range(SLOTS):
        go(remote(b0.at[yh, q], b1.at[yh, q], zs.at[q], zr.at[q], below))

    for g in (1, 2):
        @pl.when(holders[g])
        def _():
            at = panels[g].at[chunk, section - 1 if g == 1 else 0]
            mine = pltpu.make_async_copy(blocks.at[chunk], at, local_sem.at[3])
            mine.start()
            ma[section] = meta[...]
            mine.wait()

    def from_here(s):
        return ((z + s) % 16 if s < 3 else (z + 2) % 16) // 2 % 2 == yl

    def cross(s):
        return remote(panel(chunk, s), panel(chunk, s), ks.at[s], kr.at[s], opposite)

    def panel_lists(s):
        def arrived():
            remote(meta, ma.at[s], rms.at[0], rmr.at[s], partner).wait_recv()

        if s < 3:
            pl.when(section != s)(arrived)
        else:
            arrived()

    def panel_cross(s):
        @pl.when(from_here(s))
        def _():
            def arrived():
                remote(blocks.at[0], panel(0, s), rs.at[0], rr.at[s], partner).wait_recv()

            if s < 3:
                pl.when(section != s)(arrived)
            else:
                arrived()
            cross(s).start()

    def part(b, g):
        return panels[g].at[b]

    def panel_spread(g):
        for s in ((3,), (1, 2), (0,))[g]:
            @pl.when(jnp.logical_not(from_here(s)))
            def _():
                cross(s).wait_recv()
        for d in range(1, 4):
            go(remote(part(chunk, g), part(chunk, g), gs.at[g, d], gr.at[g, d], line[d - 1]), g)
        go(remote(part(chunk, g), part(chunk, g), cs.at[g, 0], cr.at[g, 0], twin), g)

    def panel_twin(g):
        for d in range(1, 4):
            b = (x + 4 - d) % 4 * 2 + core
            remote(part(b, g), part(b, g), gs.at[g, d], gr.at[g, d], twin).wait_recv()
            go(remote(part(b, g), part(b, g), cs.at[g, d], cr.at[g, d], twin), g)

    def panel_whole(g):
        for d in range(4):
            b = (x + 4 - d) % 4 * 2 + 1 - core
            remote(part(b, g), part(b, g), cs.at[g, d], cr.at[g, d], twin).wait_recv()

    def partner_block(ref, q, first):
        remote(ref.at[other, q], ref.at[other, q], ys.at[first + q], yr.at[first + q], partner).wait_recv()

    def from_both(q):
        return remote(b1.at[other, q], b2.at[other, q], zs.at[24 + q], zr.at[24 + q], below)

    n = SLOTS
    to_scalars = pltpu.make_async_copy(table, table_s, local_sem.at[4])

    def match():
        for i in range(3):
            remote(meta, mb.at[i, other], mys.at[i], myr.at[i], partner).wait_recv()
        remote(meta, mc, mus, mur, above).wait_recv()
        for s in range(SECTIONS):
            panel_lists(s)
        lane = lax.broadcasted_iota(jnp.int32, (n, n), 1)
        diag = lax.broadcasted_iota(jnp.int32, (n, n), 0) == lane

        def upright(values):
            wide = jnp.broadcast_to(values, (n, n))
            return jnp.sum(jnp.where(diag, wide, 0), axis=1, keepdims=True)

        for s, (lists, i) in enumerate(((meta, 0), (meta, 1), (meta, 2), (mc, 2))):
            out_rows, out_cols = upright(lists[0:1, 0:n]), upright(lists[1:2, 0:n])
            a_rows, a_cols = ma[s, 0:1, 0:n], ma[s, 1:2, 0:n]
            same_row = (out_rows == a_rows) & (out_rows >= 0)
            found = jnp.full((n, n), -1, jnp.int32)
            for h in range(2):
                for q in range(n):
                    inner, b_col = mb[i, h, 0:1, q:q + 1], mb[i, h, 1:2, q:q + 1]
                    hit = (a_cols == inner + RB * h) & (out_cols == b_col) & (inner >= 0)
                    found = jnp.where(hit, h * n + q, found)
            found = jnp.where(same_row, found, -1)
            matched = jnp.where(found >= 0, 1, 0)
            rank = jnp.zeros((n, n), jnp.int32)
            for p in range(n - 1):
                rank = rank + jnp.where(lane > p, matched[:, p:p + 1], 0)
            for d in range(DEPTH):
                pick = (matched > 0) & (rank == d)
                a_at = n + jnp.sum(jnp.where(pick, lane - n, 0), axis=1, keepdims=True)
                b_at = jnp.sum(jnp.where(pick, found, 0), axis=1, keepdims=True)
                table[s * n:(s + 1) * n, d:d + 1] = a_at
                table[s * n:(s + 1) * n, DEPTH + d:DEPTH + d + 1] = b_at
        to_scalars.start()

    remote(meta, mb.at[1, yh], mzs.at[0], mzr.at[0], below).wait_recv()
    go(remote(mb.at[1, yh], mb.at[2, yh], mzs.at[1], mzr.at[1], below))
    go(remote(mb.at[1, yh], mb.at[1, yh], mys.at[1], myr.at[1], partner))
    for q in range(SLOTS):
        remote(b0.at[yh, q], b1.at[yh, q], zs.at[q], zr.at[q], below).wait_recv()
        go(remote(b1.at[yh, q], b2.at[yh, q], zs.at[8 + q], zr.at[8 + q], below), 1)
        if q < EARLY:
            across(b1, q, 16)
        if q == 6:
            panel_cross(3)
        elif EARLY <= q < EARLY + 4:
            across(b0, q + 1, 0)
    remote(meta, mb.at[2, yh], mzs.at[1], mzr.at[1], below).wait_recv()
    go(remote(mb.at[2, yh], mb.at[2, yh], mys.at[2], myr.at[2], partner))
    panel_cross(2)
    panel_cross(1)

    for q in range(SLOTS):
        remote(b1.at[yh, q], b2.at[yh, q], zs.at[8 + q], zr.at[8 + q], below).wait_recv()
        if q >= EARLY:
            across(b2, q, 8, 1)
        if q == 2:
            match()
        if q == 3:
            panel_spread(0)
        if q == 4:
            panel_spread(1)
            panel_cross(0)
    for q in range(EARLY):
        partner_block(b1, q, 16)
        go(from_both(q), 1)
    for q in range(EARLY, SLOTS):
        across(b1, q, 16, 2)
    across(b0, SLOTS - 1, 0, 2)
    panel_spread(2)
    panel_twin(0)
    panel_whole(0)
    to_scalars.wait()

    def halves(v):
        high = v.astype(BF16)
        return high, (v - high.astype(F32)).astype(BF16)

    def product(s, t, b_ref):
        lefts, rights = [], []
        for d in range(DEPTH):
            a = panels[places[s][0]][table_s[s * n + t, d], places[s][1]]
            at = table_s[s * n + t, DEPTH + d]
            b = b_ref[at // n, at % n]
            lefts += halves(a)
            wide = jnp.concatenate(halves(b), axis=1)
            rights += [wide, wide]
        both = jnp.dot(jnp.concatenate(lefts, axis=1), jnp.concatenate(rights, axis=0), preferred_element_type=F32)
        return both[:, :BS] + both[:, BS:]

    def down(t):
        return remote(c_down.at[t], c_in.at[t], zs.at[16 + t], zr.at[16 + t], below)

    def sent(when):
        for copy in sends[when]:
            copy.wait_send()

    each_root_list(lambda copy: copy.wait_send())
    each_root_copy(lambda copy: copy.wait_send())
    sent(0)
    for q in range(EARLY, SLOTS):
        partner_block(b2, q, 8)
    for q in range(EARLY):
        from_both(q).wait_recv()

    def last_section(i, carry):
        c_down[2 * i], c_down[2 * i + 1] = product(3, 2 * i, b2), product(3, 2 * i + 1, b2)
        down(2 * i).start()
        down(2 * i + 1).start()
        return carry

    lax.fori_loop(0, SLOTS // 2, last_section, 0)
    panel_twin(1)
    panel_whole(1)

    def section_two(i, carry):
        acc[2 * i], acc[2 * i + 1] = product(2, 2 * i, b2), product(2, 2 * i + 1, b2)
        return carry

    lax.fori_loop(0, SLOTS // 2, section_two, 0)
    panel_twin(2)
    for s in range(SECTIONS):
        @pl.when(from_here(s))
        def _():
            cross(s).wait_send()
    sent(1)
    panel_whole(2)
    for q in range(SLOTS):
        partner_block(b0, q, 0)

    for q in range(EARLY, SLOTS):
        partner_block(b1, q, 16)

    def sections_zero_one(i, carry):
        first, second = 2 * i, 2 * i + 1
        acc[first], acc[second] = (
            acc[first] + product(0, first, b0) + product(1, first, b1),
            acc[second] + product(0, second, b0) + product(1, second, b1),
        )
        return carry

    lax.fori_loop(0, SLOTS // 2, sections_zero_one, 0)

    def result(t):
        return pltpu.make_async_copy(acc.at[t], out.at[t], out_sem.at[t])

    def finish(t, carry):
        down(t).wait_recv()
        acc[t] += c_in[t]
        result(t).start()
        return carry

    lax.fori_loop(0, SLOTS, finish, 0)
    for t in range(SLOTS):
        down(t).wait_send()
    sent(2)
    for t in range(SLOTS):
        result(t).wait()


def body(blocks, block_rows, block_cols):
    dma = pltpu.SemaphoreType.DMA
    hbm = pl.BlockSpec(memory_space=pl.ANY)
    tile = pltpu.VMEM((2, SLOTS, BS, BS), F32)
    lists = (8, BS)
    i32 = jnp.int32
    out = pl.pallas_call(
        kernel,
        out_shape=jax.ShapeDtypeStruct((SLOTS, BS, BS), F32),
        in_specs=[hbm, hbm, hbm],
        out_specs=hbm,
        scratch_shapes=[
            pltpu.VMEM((1, SLOTS), i32), pltpu.VMEM((1, SLOTS), i32),
            pltpu.VMEM(lists, i32), pltpu.VMEM((3, 2, *lists), i32), pltpu.VMEM((SECTIONS, *lists), i32),
            pltpu.VMEM(lists, i32),
            tile, tile, tile,
            *(pltpu.VMEM((SLOTS + 1, m, BS, BS), F32) for m in (1, 2, 1)),
            pltpu.VMEM((SLOTS, BS, BS), F32), pltpu.VMEM((SLOTS, BS, BS), F32), pltpu.VMEM((SLOTS, BS, BS), F32),
            pltpu.VMEM((SECTIONS * SLOTS, BS), i32), pltpu.SMEM((SECTIONS * SLOTS, BS), i32),
            dma((5,)), pltpu.SemaphoreType.REGULAR,
            dma((32,)), dma((32,)), dma((24,)), dma((24,)),
            dma((2,)), dma((2,)), dma((3,)), dma((3,)), dma(()), dma(()),
            dma((SLOTS,)), dma((4,)), dma((16,)), dma((4,)), dma((4,)), dma((4,)),
            dma((3, 4)), dma((3, 4)), dma((3, 4)), dma((3, 4)), dma((SLOTS,)),
        ],
        compiler_params=pltpu.CompilerParams(
            collective_id=0, has_side_effects=True, vmem_limit_bytes=53 * 2**20
        ),
        name="four_sections",
    )(blocks[0, 0], block_rows[0], block_cols[0])
    return out[None, None]


def solution(mesh):
    return jax.shard_map(
        body,
        mesh=mesh,
        in_specs=(P("row", "col", None, None, None), P("row", "col", None), P("row", "col", None)),
        out_specs=P("row", "col", None, None, None),
        check_vma=False,
    )
```
